512 devices in a mesh: dom: 32 (over y, x), edge: 16 (over z, core).
Axes of the slice: x: 4, y: 8, z: 8, core: 2. Of those that a mesh axis runs over, the one named last changes fastest.
Arguments:
- left_rows: float32 [131072, 400], P(('dom', 'edge')), may hold values from -1.8 to 1.8
- left_state: float32 [131072], P(('dom', 'edge')), may hold values from 0.001 to 0.1
- right_rows: float32 [131072, 400], P(('dom', 'edge')), may hold values from -1.8 to 1.8
- right_state: float32 [131072], P(('dom', 'edge')), may hold values from 0.001 to 0.1
- relation: float32 [400], replicated, may hold values from -4 to 4
- left_rows_wanted: int32 [8192, 128], P(('dom', 'edge')), may hold values from 0 to 255
- right_rows_wanted: int32 [8192, 128], P(('dom', 'edge')), may hold values from 0 to 255
- left_edge_position: int32 [512, 1024], P(('dom', 'edge')), may hold values from 0 to 2047
- right_edge_position: int32 [512, 1024], P(('dom', 'edge')), may hold values from 0 to 2047
- negative_position: int32 [512, 512], P(('dom', 'edge')), may hold values from 0 to 2047
Outputs:
- new_left: float32 [131072, 400], P(('dom', 'edge'))
- new_left_state: float32 [131072], P(('dom', 'edge'))
- new_right: float32 [131072, 400], P(('dom', 'edge'))
- new_right_state: float32 [131072], P(('dom', 'edge'))
The draws below stay inside these ranges and needn't reach their ends.
Inputs may be any that keep to these rules, and one draw needn't show every extreme that they name: `left_rows_wanted`: rows of the owner's 256 rows of a partition; one list may name a row more than once. `right_rows_wanted`: rows of the owner's 256 rows of a partition; one list may name a row more than once. `left_edge_position`: slot o * 128 + c is entry c of the list sent to owner o. `right_edge_position`: slot o * 128 + c is entry c of the list sent to owner o. `negative_position`: slot o * 128 + c is entry c of the list sent to owner o.
All inputs are finite; a program needn't handle non-finite values.
Results may differ from the reference program's by a relative error of at most 0.0036.
Values may be sent and summed in bfloat16 or wider, within the bound.
A program may use at most 64 MiB of HBM per device.

```python
import math
import jax
import jax.numpy as jnp
from jax import lax

D = 400
ROWS = 256
OWNER_ROW_LIMIT = 128
EDGE_BATCHES = 1
BATCH_EDGES = 1024
NEGATIVE_ROWS = 512
DEVICE_COUNT = 512
FETCHED_ROWS = 2048
N_EDGE = 16


def touch_ends(drawn, stream_key, smallest, top_value):
    longest = drawn.shape.index(max(drawn.shape))
    spots = []
    for shift in (0, 1):
        where = [jax.random.randint(jax.random.fold_in(stream_key, axis), (), 0, length) for axis, length in enumerate(drawn.shape)]
        where[longest] = (where[longest] + shift) % drawn.shape[longest]
        spots.append(tuple(where))
    return drawn.at[spots[0]].set(smallest).at[spots[1]].set(top_value)


def shard_levels(own_key, shape, shards, low, top_value):
    gain, own = 1.0, jax.random.fold_in(own_key, 6)
    for axis_at, shards_of in shards:
        steps = jnp.exp(jax.random.uniform(jax.random.fold_in(own, axis_at), (shards_of,), jnp.float32, low / len(shards), top_value / len(shards)))
        gain = gain * jnp.repeat(steps, shape[axis_at] // shards_of).reshape([-1 if axis == axis_at else 1 for axis in range(len(shape))])
    return gain


def gaussian(rng, extent, spread, reach, shards=(), held_as=jnp.bfloat16):
    array = spread * jax.random.normal(rng, extent, jnp.float32)
    if shards:
        array = array * shard_levels(rng, extent, shards, -0.22, 0.18)
    return jnp.clip(array, -reach, reach).astype(held_as)


def setup_inputs(seed: int = 0) -> dict:
    key_list = jax.random.split(jax.random.key(seed), 11)
    return {
        "left_rows": gaussian(key_list[0], (DEVICE_COUNT * ROWS, D), 0.3, 1.8, ((0, 512),), jnp.float32),
        "left_state": jnp.clip(jnp.exp(math.log(0.1) - 4.6051702 * jax.random.uniform(key_list[1], (DEVICE_COUNT * ROWS,), jnp.float32) ** shard_levels(key_list[1], (DEVICE_COUNT * ROWS,), ((0, 512),), -0.2, 0.2)), 0.001, 0.1),
        "right_rows": gaussian(key_list[2], (DEVICE_COUNT * ROWS, D), 0.3, 1.8, ((0, 512),), jnp.float32),
        "right_state": jnp.clip(jnp.exp(math.log(0.1) - 4.6051702 * jax.random.uniform(key_list[3], (DEVICE_COUNT * ROWS,), jnp.float32) ** shard_levels(key_list[3], (DEVICE_COUNT * ROWS,), ((0, 512),), -0.2, 0.2)), 0.001, 0.1),
        "relation": gaussian(key_list[4], (D,), 1.0, 4.0, (), jnp.float32),
        "left_rows_wanted": touch_ends(jax.random.randint(key_list[5], (DEVICE_COUNT * N_EDGE, OWNER_ROW_LIMIT), 0, ROWS), jax.random.fold_in(key_list[5], 1), 0, ROWS - 1).astype(jnp.int32),
        "right_rows_wanted": touch_ends(jax.random.randint(key_list[6], (DEVICE_COUNT * N_EDGE, OWNER_ROW_LIMIT), 0, ROWS), jax.random.fold_in(key_list[6], 1), 0, ROWS - 1).astype(jnp.int32),
        "left_edge_position": touch_ends(jax.random.randint(key_list[7], (DEVICE_COUNT * EDGE_BATCHES, BATCH_EDGES), 0, FETCHED_ROWS), jax.random.fold_in(key_list[7], 1), 0, FETCHED_ROWS - 1).astype(jnp.int32),
        "right_edge_position": touch_ends(jax.random.randint(key_list[8], (DEVICE_COUNT * EDGE_BATCHES, BATCH_EDGES), 0, FETCHED_ROWS), jax.random.fold_in(key_list[8], 1), 0, FETCHED_ROWS - 1).astype(jnp.int32),
        "negative_position": touch_ends(jax.random.randint(key_list[9], (DEVICE_COUNT * EDGE_BATCHES, NEGATIVE_ROWS), 0, FETCHED_ROWS), jax.random.fold_in(key_list[9], 1), 0, FETCHED_ROWS - 1).astype(jnp.int32),
    }


LEARN_RATE = 0.1
ADA_EPS = 1e-10

def complex_times(row_block, relation, sign_flip):
    half_width = row_block.shape[1] // 2
    re_rel = relation[:half_width]
    im_rel = sign_flip * relation[half_width:]
    re_row = row_block[:, :half_width]
    im_row = row_block[:, half_width:]
    return jnp.concatenate([re_row * re_rel - im_row * im_rel, re_row * im_rel + im_row * re_rel], axis=1)

def slot_grads(left_slots, right_slots, left_edge_position, right_edge_position, negative_position, relation):
    slot_count, row_width = left_slots.shape
    grad_left = jnp.zeros((slot_count, row_width), jnp.float32)
    grad_right = jnp.zeros((slot_count, row_width), jnp.float32)
    neg_count = negative_position.shape[1]
    for batch_index in range(left_edge_position.shape[0]):
        left_idx = left_edge_position[batch_index]
        right_idx = right_edge_position[batch_index]
        neg_idx = negative_position[batch_index]
        left_take = jnp.take(left_slots, left_idx, axis=0).astype(jnp.float32)
        query_rows = complex_times(left_take, relation, 1.0).astype(jnp.bfloat16)
        target = jnp.take(right_slots, right_idx, axis=0)
        sampled = jnp.take(right_slots, neg_idx, axis=0)
        positive = lax.optimization_barrier(jnp.sum(query_rows.astype(jnp.float32) * target.astype(jnp.float32), axis=1))
        negative = lax.dot_general(query_rows, sampled, (((1,), (1,)), ((), ())), preferred_element_type=jnp.float32)
        pull_weight = -jax.nn.sigmoid(-positive)
        push_weight = (jax.nn.sigmoid(negative) / neg_count).astype(jnp.bfloat16)
        grad_query = pull_weight[:, None] * target.astype(jnp.float32) + jnp.dot(push_weight, sampled, preferred_element_type=jnp.float32)
        grad_left = grad_left.at[left_idx].add(complex_times(grad_query, relation, -1.0))
        grad_right = grad_right.at[right_idx].add(pull_weight[:, None] * query_rows.astype(jnp.float32))
        neg_grad = lax.dot_general(push_weight, query_rows, (((0,), (0,)), ((), ())), preferred_element_type=jnp.float32)
        grad_right = grad_right.at[neg_idx].add(neg_grad)
    return (grad_left.astype(jnp.bfloat16), grad_right.astype(jnp.bfloat16))

def adagrad(table, state, grads):
    state_new = state + lax.optimization_barrier(jnp.mean(grads * grads, axis=1))
    table_new = table - LEARN_RATE * grads / (jnp.sqrt(state_new)[:, None] + ADA_EPS)
    return (table_new, state_new)

def reference(left_rows, left_state, right_rows, right_state, relation, left_rows_wanted, right_rows_wanted, left_edge_position, right_edge_position, negative_position):
    row_width = left_rows.shape[1]
    group_of = jnp.arange(DEVICE_COUNT, dtype=jnp.int32) // N_EDGE
    owners = jnp.arange(N_EDGE, dtype=jnp.int32)
    starting_row = (group_of[:, None] * N_EDGE + owners[None, :]) * ROWS
    left_entity_index = (starting_row[:, :, None] + left_rows_wanted.reshape(DEVICE_COUNT, N_EDGE, OWNER_ROW_LIMIT)).reshape(DEVICE_COUNT, FETCHED_ROWS).astype(jnp.int32)
    right_entity_index = (starting_row[:, :, None] + right_rows_wanted.reshape(DEVICE_COUNT, N_EDGE, OWNER_ROW_LIMIT)).reshape(DEVICE_COUNT, FETCHED_ROWS).astype(jnp.int32)
    left_low = left_rows.astype(jnp.bfloat16)
    right_low = right_rows.astype(jnp.bfloat16)

    def per_device(items):
        left_pick, right_pick, left_edges, right_edges, neg_edges = items
        return slot_grads(jnp.take(left_low, left_pick, axis=0), jnp.take(right_low, right_pick, axis=0), left_edges, right_edges, neg_edges, relation)
    slot_left, slot_right = lax.map(per_device, (left_entity_index, right_entity_index, left_edge_position.reshape(DEVICE_COUNT, EDGE_BATCHES, BATCH_EDGES), right_edge_position.reshape(DEVICE_COUNT, EDGE_BATCHES, BATCH_EDGES), negative_position.reshape(DEVICE_COUNT, EDGE_BATCHES, NEGATIVE_ROWS)))
    grad_left = jnp.zeros(left_rows.shape, jnp.float32).at[left_entity_index.reshape(-1)].add(slot_left.astype(jnp.float32).reshape(-1, row_width))
    grad_right = jnp.zeros(right_rows.shape, jnp.float32).at[right_entity_index.reshape(-1)].add(slot_right.astype(jnp.float32).reshape(-1, row_width))
    new_left, new_left_state = adagrad(left_rows, left_state, grad_left)
    upd_right, upd_state = adagrad(right_rows, right_state, grad_right)
    step_rows = N_EDGE * ROWS
    return (new_left, new_left_state, jnp.roll(upd_right, step_rows, axis=0), jnp.roll(upd_state, step_rows, axis=0))
```

```python
import functools

import jax
import jax.numpy as jnp
from jax import lax
from jax.experimental import pallas as pl
from jax.experimental.pallas import tpu as pltpu
from jax.sharding import PartitionSpec as P

LEARN_RATE = 0.1
ADA_EPS = 1e-10
MESH = pl.DeviceIdType.MESH
F32 = jnp.float32
BF16 = jnp.bfloat16

LEFT, RIGHT = 0, 1
HOPS = ((4, 3), (3, 4))
LANES = 128


def kernel(
    left_ref, left_state_ref, right_ref, right_state_ref, relation_ref,
    left_wanted_ref, right_wanted_ref, left_pos_ref, right_pos_ref, neg_pos_ref,
    new_left_ref, new_left_state_ref, new_right_ref, new_right_state_ref,
    tab,
    hot_left,
    hot_right,
    key_left,
    key_right,
    keyt_left,
    keyt_right,
    got_left,
    got_right,
    rel_col,
    query,
    neg_t,
    neg,
    push,
    pull,
    grad_left,
    grad_right,
    ring_out,
    ring_in,
    pair_out,
    pair_in,
    own_out,
    own_in,
    rows_in,
    state_in,
    ag_send, ag_recv, agp_send, agp_recv,
    rs_send, rs_recv, rsp_send, rsp_recv,
    misc_send, misc_recv,
):
    width, rows = left_ref.shape
    half = width // 2
    edges = left_pos_ref.shape[1]
    negs = neg_pos_ref.shape[1]
    doms = lax.axis_size("dom")
    owners = lax.axis_size("edge")
    chips = owners // 2
    dom = lax.axis_index("dom")
    me = lax.axis_index("edge")
    z = me // 2
    core = lax.rem(me, 2)
    partner = z * 2 + (1 - core)
    ring = (lax.rem(me + 2, owners), lax.rem(me + owners - 2, owners))
    next_dom = lax.rem(dom + 1, doms)
    prev_dom = lax.rem(dom + doms - 1, doms)

    barrier = pltpu.get_barrier_semaphore()
    for d, e in (
        (dom, partner), (dom, ring[0]), (dom, ring[1]),
        (prev_dom, me), (prev_dom, ring[0]), (prev_dom, ring[1]),
    ):
        pl.semaphore_signal(barrier, inc=1, device_id=(d, e), device_id_type=MESH)

    tab[LEFT, z, core] = left_ref[...].astype(BF16)
    tab[RIGHT, z, core] = right_ref[...].astype(BF16)
    pl.semaphore_wait(barrier, 6)

    started = []

    def send(src, dst, send_sem, recv_sem, d, e):
        copy = pltpu.make_async_remote_copy(
            src_ref=src, dst_ref=dst, send_sem=send_sem, recv_sem=recv_sem,
            device_id=(d, e), device_id_type=MESH,
        )
        copy.start()
        started.append(copy)
        return copy

    def at_chip(offset):
        return lax.rem(z + offset + 2 * chips, chips)

    def ring_gather(t, way, step):
        offset = -(step - 1) if way == 0 else step - 1
        block = tab.at[t, at_chip(offset), core]
        return send(block, block, ag_send.at[t, way, step - 1], ag_recv.at[t, way, step - 1], dom, ring[way])

    def pair_gather(t, slot, offset):
        block = tab.at[t, at_chip(offset), core]
        return send(block, block, agp_send.at[t, slot], agp_recv.at[t, slot], dom, partner)

    ring_copy = {}
    pair_copy = {}
    for t in (LEFT, RIGHT):
        for way in (0, 1):
            ring_copy[t, way, 1] = ring_gather(t, way, 1)
        pair_copy[t, 0] = pair_gather(t, 0, 0)
    rows_copy = send(right_ref, rows_in, misc_send.at[0], misc_recv.at[0], next_dom, me)
    state_copy = send(right_state_ref, state_in, misc_send.at[1], misc_recv.at[1], next_dom, me)

    def place(pos, wanted_ref):
        count = pos.shape[1]
        col = lax.broadcasted_iota(jnp.int32, (LANES, count), 0)
        hot = jnp.where(col == lax.rem(pos, LANES), 1.0, 0.0).astype(BF16)
        by_owner = jnp.dot(wanted_ref[...].astype(F32).astype(BF16), hot, preferred_element_type=F32)
        owner = pos // LANES
        own = lax.broadcasted_iota(jnp.int32, (owners, count), 0)
        row = jnp.sum(jnp.where(own == owner, by_owner, 0.0), axis=0, keepdims=True)
        return owner.astype(F32) * float(rows) + row

    def fill_keys(key, start, count, keyt, key_ref):
        key_ref[:, pl.ds(start, count)] = key.astype(jnp.int32)
        keyt[pl.ds(start, count), :] = jnp.transpose(jnp.broadcast_to(key, (LANES, count))).astype(jnp.int32)

    fill_keys(place(left_pos_ref[...], left_wanted_ref), 0, edges, keyt_left, key_left)
    fill_keys(place(right_pos_ref[...], right_wanted_ref), 0, edges, keyt_right, key_right)
    fill_keys(place(neg_pos_ref[...], right_wanted_ref), edges, negs, keyt_right, key_right)

    row_at = lax.broadcasted_iota(jnp.int32, (width, width), 0)
    col_at = lax.broadcasted_iota(jnp.int32, (width, width), 1)
    col = jnp.sum(jnp.where(row_at == col_at, relation_ref[...], 0.0), axis=1, keepdims=True)
    rel_col[...] = jnp.broadcast_to(col, (width, LANES))

    def fill_hot(hot, keyt, chip):
        count = keyt.shape[0]

        def step(i, _):
            at = pl.ds(pl.multiple_of(i * 256, 256), 256)
            lane = lax.broadcasted_iota(jnp.int32, (256, LANES), 1)
            for c in (0, 1):
                local = keyt[at, :] - (chip * 2 + c) * rows
                for h in range(rows // LANES):
                    hot[chip, c, at, pl.ds(h * LANES, LANES)] = jnp.where(
                        lane + h * LANES == local, 1.0, 0.0
                    ).astype(BF16)
            return 0

        lax.fori_loop(0, count // 256, step, 0)

    TILE = 512

    def take(t, chip, first):
        key_ref, got = ((key_left, got_left), (key_right, got_right))[t]
        count = key_ref.shape[1]

        def step(i, _):
            at = pl.ds(pl.multiple_of(i * TILE, TILE), TILE)
            part = None
            for c in (0, 1):
                local = key_ref[:, at] - (chip * 2 + c) * rows
                row = lax.broadcasted_iota(jnp.int32, (rows, TILE), 0)
                hot = jnp.where(row == local, 1.0, 0.0).astype(BF16)
                term = jnp.dot(tab[t, chip, c], hot, preferred_element_type=F32)
                part = term if part is None else part + term
            if first:
                got[:, at] = part
            else:
                got[:, at] += part
            return 0

        lax.fori_loop(0, count // TILE, step, 0)

    def arrive(t, step):
        for way in (0, 1):
            if step > HOPS[t][way]:
                continue
            ring_copy[t, way, step].wait_recv()
            if step < HOPS[t][way]:
                ring_copy[t, way, step + 1] = ring_gather(t, way, step + 1)
            slot = step if way == 0 else chips - step
            pair_copy[t, slot] = pair_gather(t, slot, -step if way == 0 else step)

    for chip in range(chips):
        fill_hot(hot_left, keyt_left, chip)
        fill_hot(hot_right, keyt_right, chip)
    for step in range(0, chips // 2 + 1):
        for t in (LEFT, RIGHT):
            if step > 0:
                arrive(t, step)
        for t in (LEFT, RIGHT):
            for way in (0, 1):
                if step > HOPS[t][way] or (step == 0 and way == 1):
                    continue
                offset = -step if way == 0 else step
                slot = step if way == 0 else chips - step
                pair_copy[t, slot].wait_recv()
                take(t, at_chip(offset), step == 0)

    def score(i, _):
        at = pl.ds(pl.multiple_of(i * LANES, LANES), LANES)
        pr = rel_col[:half, :]
        pi = rel_col[half:, :]
        lr = got_left[:half, at]
        li = got_left[half:, at]
        q = jnp.concatenate([lr * pr - li * pi, lr * pi + li * pr], axis=0).astype(BF16)
        query[:, at] = q
        q = q.astype(F32)
        positive = jnp.sum(q * got_right[:, at], axis=0, keepdims=True)
        weight = -jax.nn.sigmoid(-positive)
        pull[:, at] = weight
        grad_right[:, at] = (weight * q).astype(BF16)
        return 0

    lax.fori_loop(0, edges // LANES, score, 0)
    neg_cols = pl.ds(edges, negs)
    neg_t[...] = got_right[:, neg_cols].astype(BF16)
    neg[...] = jnp.transpose(got_right[:, neg_cols]).astype(BF16)

    def negatives(i, _):
        at = pl.ds(pl.multiple_of(i * 256, 256), 256)
        negative = jnp.dot(neg[...], query[:, at], preferred_element_type=F32)
        push[:, at] = (jax.nn.sigmoid(negative) * (1.0 / negs)).astype(BF16)
        return 0

    lax.fori_loop(0, edges // 256, negatives, 0)
    grad_right[:, neg_cols] = lax.dot_general(
        query[...], push[...], (((1,), (1,)), ((), ())), preferred_element_type=F32
    ).astype(BF16)

    def left_grads():
        def step(i, _):
            at = pl.ds(pl.multiple_of(i * LANES, LANES), LANES)
            pr = rel_col[:half, :]
            pi = rel_col[half:, :]
            g = pull[:, at] * got_right[:, at] + jnp.dot(neg_t[...], push[:, at], preferred_element_type=F32)
            gr = g[:half, :]
            gi = g[half:, :]
            grad_left[:, at] = jnp.concatenate([gr * pr + gi * pi, gi * pr - gr * pi], axis=0).astype(BF16)
            return 0

        lax.fori_loop(0, edges // LANES, step, 0)

    def dense(t, chip, c):
        grad, hot = ((grad_left, hot_left), (grad_right, hot_right))[t]
        return jnp.dot(grad[...], hot[chip, c], preferred_element_type=F32)

    def for_pair(t, offset):
        chip = at_chip(offset)
        slot = offset % chips
        pair_out[t, slot] = dense(t, chip, 1 - core).astype(BF16)
        pair_copy[t, slot] = send(
            pair_out.at[t, slot], pair_in.at[t, slot], rsp_send.at[t, slot], rsp_recv.at[t, slot], dom, partner
        )

    def own_part(t, offset):
        slot = offset % chips
        part = dense(t, at_chip(offset), core)
        pair_copy[t, slot].wait_recv()
        return part + pair_in[t, slot].astype(F32)

    def offset_of(t, way, step):
        far = HOPS[t][way] - step + 1
        return far if way == 0 else -far

    rs_copy = {}

    def pass_on(t, way, step):
        part = own_part(t, offset_of(t, way, step))
        if step > 1:
            rs_copy[t, way, step - 1].wait_recv()
            part = part + ring_in[t, way, step - 2].astype(F32)
        ring_out[t, way, step - 1] = part.astype(BF16)
        last = t == RIGHT and step == HOPS[t][way]
        rs_copy[t, way, step] = send(
            ring_out.at[t, way, step - 1], ring_in.at[t, way, step - 1],
            rs_send.at[t, way, step - 1], rs_recv.at[t, way, step - 1],
            next_dom if last else dom, ring[way],
        )

    for step in range(1, chips // 2 + 1):
        for t in (RIGHT, LEFT):
            if t == LEFT and step == 1:
                left_grads()
            ways = [way for way in (0, 1) if step <= HOPS[t][way]]
            for way in ways:
                for_pair(t, offset_of(t, way, step))
            for way in ways:
                pass_on(t, way, step)
    for_pair(RIGHT, 0)
    for_pair(LEFT, 0)
    own_out[...] = own_part(RIGHT, 0).astype(BF16)
    own_copy = send(own_out, own_in, misc_send.at[2], misc_recv.at[2], next_dom, me)

    def adagrad(row, state, grad, new_row_ref, new_state_ref):
        new_state = state + jnp.sum(grad * grad, axis=0, keepdims=True) * (1.0 / width)
        new_state_ref[...] = new_state
        new_row_ref[...] = row - LEARN_RATE * grad / (jnp.sqrt(new_state) + ADA_EPS)

    def from_ring(t):
        total = None
        for way in (0, 1):
            step = HOPS[t][way]
            rs_copy[t, way, step].wait_recv()
            part = ring_in[t, way, step - 1].astype(F32)
            total = part if total is None else total + part
        return total

    left_total = own_part(LEFT, 0) + from_ring(LEFT)
    adagrad(left_ref[...], left_state_ref[...], left_total, new_left_ref, new_left_state_ref)
    rows_copy.wait_recv()
    state_copy.wait_recv()
    own_copy.wait_recv()
    right_total = own_in[...].astype(F32) + from_ring(RIGHT)
    adagrad(rows_in[...], state_in[...], right_total, new_right_ref, new_right_state_ref)
    for copy in started:
        copy.wait_send()


def body(
    left_rows, left_state, right_rows, right_state, relation,
    left_rows_wanted, right_rows_wanted,
    left_edge_position, right_edge_position, negative_position,
):
    rows, width = left_rows.shape
    edges = left_edge_position.shape[1]
    negs = negative_position.shape[1]
    chips = lax.axis_size("edge") // 2
    both = edges + negs
    vmem = pl.BlockSpec(memory_space=pltpu.VMEM)
    dma = pltpu.SemaphoreType.DMA
    block = (width, rows)
    new_left, new_left_state, new_right, new_right_state = pl.pallas_call(
        kernel,
        out_shape=(
            jax.ShapeDtypeStruct(block, F32),
            jax.ShapeDtypeStruct((1, rows), F32),
            jax.ShapeDtypeStruct(block, F32),
            jax.ShapeDtypeStruct((1, rows), F32),
        ),
        in_specs=[vmem] * 10,
        out_specs=(vmem,) * 4,
        scratch_shapes=[
            pltpu.VMEM((2, chips, 2) + block, BF16),
            pltpu.VMEM((chips, 2, edges, rows), BF16),
            pltpu.VMEM((chips, 2, both, rows), BF16),
            pltpu.VMEM((1, edges), jnp.int32),
            pltpu.VMEM((1, both), jnp.int32),
            pltpu.VMEM((edges, LANES), jnp.int32),
            pltpu.VMEM((both, LANES), jnp.int32),
            pltpu.VMEM((width, edges), F32),
            pltpu.VMEM((width, both), F32),
            pltpu.VMEM((width, LANES), F32),
            pltpu.VMEM((width, edges), BF16),
            pltpu.VMEM((width, negs), BF16),
            pltpu.VMEM((negs, width), BF16),
            pltpu.VMEM((negs, edges), BF16),
            pltpu.VMEM((1, edges), F32),
            pltpu.VMEM((width, edges), BF16),
            pltpu.VMEM((width, both), BF16),
            pltpu.VMEM((2, 2, chips // 2) + block, BF16),
            pltpu.VMEM((2, 2, chips // 2) + block, BF16),
            pltpu.VMEM((2, chips) + block, BF16),
            pltpu.VMEM((2, chips) + block, BF16),
            pltpu.VMEM(block, BF16),
            pltpu.VMEM(block, BF16),
            pltpu.VMEM(block, F32),
            pltpu.VMEM((1, rows), F32),
            dma((2, 2, chips // 2)), dma((2, 2, chips // 2)), dma((2, chips)), dma((2, chips)),
            dma((2, 2, chips // 2)), dma((2, 2, chips // 2)), dma((2, chips)), dma((2, chips)),
            dma((3,)), dma((3,)),
        ],
        compiler_params=pltpu.CompilerParams(
            collective_id=0, has_side_effects=True, vmem_limit_bytes=62 * 1024 * 1024
        ),
        name="bucket_round",
    )(
        left_rows.T, left_state.reshape(1, rows), right_rows.T, right_state.reshape(1, rows),
        relation.reshape(1, width), left_rows_wanted, right_rows_wanted,
        left_edge_position, right_edge_position, negative_position,
    )
    return (new_left.T, new_left_state.reshape(rows), new_right.T, new_right_state.reshape(rows))


def solution(mesh):
    split = P(("dom", "edge"), None)
    return jax.shard_map(
        body,
        mesh=mesh,
        in_specs=(split, P(("dom", "edge")), split, P(("dom", "edge")), P(), split, split, split, split, split),
        out_specs=(split, P(("dom", "edge")), split, P(("dom", "edge"))),
        check_vma=False,
    )
```

```python
import jax
import jax.numpy as jnp
from jax import lax
from jax.experimental import pallas as pl
from jax.experimental.pallas import tpu as pltpu
from jax.sharding import PartitionSpec as P

LEARN_RATE = 0.1
ADA_EPS = 1e-10
MESH = pl.DeviceIdType.MESH
F32 = jnp.float32
BF16 = jnp.bfloat16

LEFT, RIGHT = 0, 1
HOPS = ((4, 3), (3, 4))
LANES = 128
STRIP = 256
CUT = 208


def round_kernel(
    left_hbm, right_hbm, right_state_hbm, relation_hbm,
    left_wanted_hbm, right_wanted_hbm, left_pos_hbm, right_pos_hbm, neg_pos_hbm,
    total_left, total_right, rows_out, state_out,
    left_ref, right_ref, relation_ref, left_wanted_ref, right_wanted_ref,
    left_pos_ref, right_pos_ref, neg_pos_ref,
    tab,
    hot_left,
    hot_right,
    key_left,
    key_right,
    keyt_left,
    keyt_right,
    got_left,
    got_right,
    rel_col,
    query,
    query_rows,
    neg_t,
    push,
    pull,
    grad_left,
    grad_right,
    mine,
    ring_out,
    ring_in,
    pair_out,
    pair_in,
    own_out,
    own_in,
    load_sem, ag_send, ag_recv, agp_send, agp_recv,
    rs_send, rs_recv, rsp_send, rsp_recv,
    misc_send, misc_recv,
):
    width, rows = left_ref.shape
    half = width // 2
    edges = left_pos_ref.shape[1]
    negs = neg_pos_ref.shape[1]
    doms = lax.axis_size("dom")
    owners = lax.axis_size("edge")
    chips = owners // 2
    far = chips // 2
    dom = lax.axis_index("dom")
    me = lax.axis_index("edge")
    z = me // 2
    core = lax.rem(me, 2)
    partner = z * 2 + (1 - core)
    ring = (lax.rem(me + 2, owners), lax.rem(me + owners - 2, owners))
    next_dom = lax.rem(dom + 1, doms)
    prev_dom = lax.rem(dom + doms - 1, doms)

    barrier = pltpu.get_barrier_semaphore()
    for d, e in (
        (dom, partner), (dom, ring[0]), (dom, ring[1]),
        (prev_dom, me), (prev_dom, ring[0]), (prev_dom, ring[1]),
    ):
        pl.semaphore_signal(barrier, inc=1, device_id=(d, e), device_id_type=MESH)

    loads = [
        pltpu.make_async_copy(src, dst, load_sem.at[i])
        for i, (src, dst) in enumerate((
            (left_hbm, left_ref), (right_hbm, right_ref), (relation_hbm, relation_ref),
            (left_wanted_hbm, left_wanted_ref), (right_wanted_hbm, right_wanted_ref),
            (left_pos_hbm, left_pos_ref), (right_pos_hbm, right_pos_ref), (neg_pos_hbm, neg_pos_ref),
        ))
    ]
    for load in loads:
        load.start()
    loads[0].wait()
    tab[LEFT, z, core] = left_ref[...].astype(BF16)
    pl.semaphore_wait(barrier, 6)

    started = []

    def send(src, dst, send_sem, recv_sem, d, e):
        copy = pltpu.make_async_remote_copy(
            src_ref=src, dst_ref=dst, send_sem=send_sem, recv_sem=recv_sem,
            device_id=(d, e), device_id_type=MESH,
        )
        copy.start()
        started.append(copy)
        return copy

    def at_chip(offset):
        return lax.rem(z + offset + 2 * chips, chips)

    PARTS = (pl.ds(0, CUT), pl.ds(CUT, width - CUT))
    ring_copy = {}
    pair_copy = {}

    def piece(t, offset, part):
        block = tab.at[t, at_chip(offset), core]
        return block if part is None else block.at[PARTS[part]]

    def ring_gather(t, way, step, part=None):
        block = piece(t, -(step - 1) if way == 0 else step - 1, part)
        sem = (t, way, step - 1, part or 0)
        ring_copy[t, way, step, part] = send(block, block, ag_send.at[sem], ag_recv.at[sem], dom, ring[way])

    def pair_gather(t, offset, part=None):
        block = piece(t, offset, part)
        sem = (t, offset % chips, part or 0)
        copy = send(block, block, agp_send.at[sem], agp_recv.at[sem], dom, partner)
        pair_copy.setdefault((t, offset % chips), []).append(copy)

    def arrive(t, step, turn=None):
        parts = [None if turn is None else (way + turn) % 2 for way in (0, 1)]
        for way in (0, 1):
            ring_copy[t, way, step, parts[way]].wait_recv()
            if step < far - 1:
                ring_gather(t, way, step + 1, parts[way])
            elif step == far - 1 and parts[way] in (None, way):
                ring_gather(t, way, far, way)
        for way in (0, 1):
            pair_gather(t, -step if way == 0 else step, parts[way])

    def from_pair(t, offset):
        for copy in pair_copy[t, offset % chips]:
            copy.wait_recv()

    for way in (0, 1):
        ring_gather(LEFT, way, 1)
    pair_gather(LEFT, 0)
    for load in loads[1:]:
        load.wait()
    tab[RIGHT, z, core] = right_ref[...].astype(BF16)

    def place(pos, wanted_ref):
        count = pos.shape[1]
        col = lax.broadcasted_iota(jnp.int32, (LANES, count), 0)
        hot = jnp.where(col == lax.rem(pos, LANES), 1.0, 0.0).astype(BF16)
        by_owner = jnp.dot(wanted_ref[...].astype(F32).astype(BF16), hot, preferred_element_type=F32)
        owner = pos // LANES
        own = lax.broadcasted_iota(jnp.int32, (owners, count), 0)
        row = jnp.sum(jnp.where(own == owner, by_owner, 0.0), axis=0, keepdims=True)
        return owner.astype(F32) * float(rows) + row

    def fill_keys(key, start, count, keyt, key_ref):
        key_ref[:, pl.ds(start, count)] = key.astype(jnp.int32)
        keyt[pl.ds(start, count), :] = jnp.transpose(jnp.broadcast_to(key, (LANES, count))).astype(jnp.int32)

    fill_keys(place(left_pos_ref[...], left_wanted_ref), 0, edges, keyt_left, key_left)
    fill_keys(place(right_pos_ref[...], right_wanted_ref), 0, edges, keyt_right, key_right)
    fill_keys(place(neg_pos_ref[...], right_wanted_ref), edges, negs, keyt_right, key_right)

    for way in (0, 1):
        ring_gather(RIGHT, way, 1, way)
    pair_gather(RIGHT, 0)
    rows_copy = send(right_ref, rows_out, misc_send.at[0], misc_recv.at[0], next_dom, me)
    state_copy = send(right_state_hbm, state_out, misc_send.at[1], misc_recv.at[1], next_dom, me)

    row_at = lax.broadcasted_iota(jnp.int32, (width, width), 0)
    col_at = lax.broadcasted_iota(jnp.int32, (width, width), 1)
    col = jnp.sum(jnp.where(row_at == col_at, relation_ref[...], 0.0), axis=1, keepdims=True)
    rel_col[...] = jnp.broadcast_to(col, (width, STRIP))

    def fill_hot(hot, keyt, chip):
        count = keyt.shape[0]

        def step(i, _):
            at = pl.ds(pl.multiple_of(i * 256, 256), 256)
            lane = lax.broadcasted_iota(jnp.int32, (256, LANES), 1)
            for c in (0, 1):
                local = keyt[at, :] - (chip * 2 + c) * rows
                for h in range(rows // LANES):
                    hot[chip, c, at, pl.ds(h * LANES, LANES)] = jnp.where(
                        lane + h * LANES == local, 1.0, 0.0
                    ).astype(BF16)
            return 0

        lax.fori_loop(0, count // 256, step, 0)

    def fill(*some):
        for chip in some:
            fill_hot(hot_left, keyt_left, chip)
            fill_hot(hot_right, keyt_right, chip)

    TILE = 512

    def take(t, offsets, first=False):
        key_ref, got = ((key_left, got_left), (key_right, got_right))[t]
        count = key_ref.shape[1]
        for offset in offsets:
            from_pair(t, offset)

        def step(i, _):
            at = pl.ds(pl.multiple_of(i * TILE, TILE), TILE)
            row = lax.broadcasted_iota(jnp.int32, (rows, TILE), 0)
            part = None
            for offset in offsets:
                chip = at_chip(offset)
                for c in (0, 1):
                    local = key_ref[:, at] - (chip * 2 + c) * rows
                    hot = jnp.where(row == local, 1.0, 0.0).astype(BF16)
                    term = jnp.dot(tab[t, chip, c], hot, preferred_element_type=F32)
                    part = term if part is None else part + term
            if first:
                got[:, at] = part
            else:
                got[:, at] += part
            return 0

        lax.fori_loop(0, count // TILE, step, 0)

    fill(0, 1, 2, 3)
    arrive(LEFT, 1)
    for way in (0, 1):
        ring_gather(RIGHT, way, 1, 1 - way)
    take(LEFT, (0,), first=True)
    take(RIGHT, (0,), first=True)
    fill(4, 5, 6, 7)
    arrive(LEFT, 2)
    arrive(RIGHT, 1, 0)
    take(LEFT, (-1, 1))
    take(LEFT, (-2, 2))
    arrive(LEFT, 3)
    arrive(RIGHT, 1, 1)
    take(RIGHT, (-1, 1))
    arrive(RIGHT, 2, 0)
    take(LEFT, (-3, 3))
    arrive(LEFT, far, 0)
    arrive(RIGHT, 2, 1)
    take(LEFT, (far,))

    def strip(i):
        return pl.ds(pl.multiple_of(i * STRIP, STRIP), STRIP)

    def make_query(i, _):
        at = strip(i)
        pr = rel_col[:half, :]
        pi = rel_col[half:, :]
        lr = got_left[:half, at]
        li = got_left[half:, at]
        q = jnp.concatenate([lr * pr - li * pi, lr * pi + li * pr], axis=0)
        query[:, at] = q.astype(BF16)
        query_rows[at, :] = jnp.transpose(q).astype(BF16)
        return 0

    lax.fori_loop(0, edges // STRIP, make_query, 0)
    arrive(RIGHT, 3, 0)
    take(RIGHT, (-2, 2))
    arrive(RIGHT, 3, 1)
    take(RIGHT, (-3, 3))
    arrive(RIGHT, far, 0)

    def last_columns(at, cores):
        chip = at_chip(far)
        row = lax.broadcasted_iota(jnp.int32, (rows, at.size), 0)
        part = got_right[:, at]
        for c in cores:
            local = key_right[:, at] - (chip * 2 + c) * rows
            hot = jnp.where(row == local, 1.0, 0.0).astype(BF16)
            part = part + jnp.dot(tab[RIGHT, chip, c], hot, preferred_element_type=F32)
        got_right[:, at] = part
        return part

    neg_cols = pl.ds(edges, negs)
    last_columns(neg_cols, (core,))
    from_pair(RIGHT, far)
    neg_t[...] = last_columns(neg_cols, (1 - core,)).astype(BF16)

    neg_total = None
    for i in range(edges // STRIP):
        at = pl.ds(i * STRIP, STRIP)
        negative = jnp.dot(query_rows[at, :], neg_t[...], preferred_element_type=F32)
        p = (jnp.tanh(negative * 0.5) * (0.5 / negs) + (0.5 / negs)).astype(BF16)
        push[at, :] = p
        term = jnp.dot(query[:, at], p, preferred_element_type=F32)
        neg_total = term if neg_total is None else neg_total + term
        q = query[:, at].astype(F32)
        positive = jnp.sum(q * last_columns(at, (0, 1)), axis=0, keepdims=True)
        weight = -jax.nn.sigmoid(-positive)
        pull[:, at] = weight
        grad_right[:, at] = (weight * q).astype(BF16)
    grad_right[:, neg_cols] = neg_total.astype(BF16)

    def left_grads():
        pr = rel_col[:half, :]
        pi = rel_col[half:, :]
        for i in range(edges // STRIP):
            at = pl.ds(i * STRIP, STRIP)
            g = pull[:, at] * got_right[:, at] + lax.dot_general(
                neg_t[...], push[at, :], (((1,), (1,)), ((), ())), preferred_element_type=F32
            )
            gr = g[:half, :]
            gi = g[half:, :]
            grad_left[:, at] = jnp.concatenate([gr * pr + gi * pi, gi * pr - gr * pi], axis=0).astype(BF16)

    def dense(t, offset, c):
        grad, hot = ((grad_left, hot_left), (grad_right, hot_right))[t]
        return jnp.dot(grad[...], hot[at_chip(offset), c], preferred_element_type=F32)

    def offset_of(t, way, step):
        left_to_go = HOPS[t][way] - step + 1
        return left_to_go if way == 0 else -left_to_go

    def ways_of(t, step):
        return [way for way in (0, 1) if step <= HOPS[t][way]]

    def give(t, offset):
        slot = offset % chips
        pair_out[t, slot] = dense(t, offset, 1 - core).astype(BF16)
        pair_copy[t, slot] = send(
            pair_out.at[t, slot], pair_in.at[t, slot], rsp_send.at[t, slot], rsp_recv.at[t, slot], dom, partner
        )

    def both_cores(t, offset):
        slot = offset % chips
        part = dense(t, offset, core)
        pair_copy[t, slot].wait_recv()
        return part + pair_in[t, slot].astype(F32)

    rs_copy = {}

    def pass_on(t, way, step, part):
        ring_out[t, way, step - 1] = part.astype(BF16)
        last = t == RIGHT and step == HOPS[t][way]
        rs_copy[t, way, step] = send(
            ring_out.at[t, way, step - 1], ring_in.at[t, way, step - 1],
            rs_send.at[t, way, step - 1], rs_recv.at[t, way, step - 1],
            next_dom if last else dom, ring[way],
        )

    def came(t, way, step):
        rs_copy[t, way, step].wait_recv()
        return ring_in[t, way, step - 1].astype(F32)

    def give_all(t, step):
        for way in ways_of(t, step):
            give(t, offset_of(t, way, step))

    def first(t):
        for way in (0, 1):
            pass_on(t, way, 1, both_cores(t, offset_of(t, way, 1)))

    def ready(t, step):
        for way in ways_of(t, step):
            mine[t, way] = both_cores(t, offset_of(t, way, step))

    def onward(t, step):
        for way in ways_of(t, step):
            pass_on(t, way, step, mine[t, way] + came(t, way, step - 1))

    give_all(RIGHT, 1)
    first(RIGHT)
    left_grads()
    give_all(LEFT, 1)
    first(LEFT)
    give_all(RIGHT, 2)
    give(RIGHT, 0)
    ready(RIGHT, 2)
    own_out[...] = both_cores(RIGHT, 0).astype(BF16)
    own_copy = send(own_out, own_in, misc_send.at[2], misc_recv.at[2], next_dom, me)
    give_all(LEFT, 2)
    for step in range(2, far + 1):
        onward(RIGHT, step)
        ready(LEFT, step)
        if step < far:
            give_all(RIGHT, step + 1)
        else:
            give(LEFT, 0)
            mine[LEFT, 1] = both_cores(LEFT, 0)
        onward(LEFT, step)
        if step < far:
            ready(RIGHT, step + 1)
            give_all(LEFT, step + 1)
    rows_copy.wait_recv()
    state_copy.wait_recv()
    own_copy.wait_recv()

    def finish(t, total):
        for way in (0, 1):
            total = total + came(t, way, HOPS[t][way])
        return total

    total_left[...] = finish(LEFT, mine[LEFT, 1])
    total_right[...] = finish(RIGHT, own_in[...].astype(F32))
    for copy in started:
        copy.wait_send()


def update_kernel(*refs):
    tables = (refs[0:3], refs[3:6])
    results = (refs[6:8], refs[8:10])
    held, made = refs[10], refs[11]
    held_state, made_state = refs[12], refs[13]
    load_sem, store_sem = refs[14], refs[15]
    width = held.shape[2]
    loads = []
    for t in (LEFT, RIGHT):
        row, state, grad = tables[t]
        loads.append([
            pltpu.make_async_copy(grad, held.at[t, 0], load_sem.at[t, 0]),
            pltpu.make_async_copy(state, held_state.at[t], load_sem.at[t, 1]),
            pltpu.make_async_copy(row, held.at[t, 1], load_sem.at[t, 2]),
        ])
        for load in loads[t]:
            load.start()
    stores = []
    for t in (LEFT, RIGHT):
        for load in loads[t]:
            load.wait()
        grad = held[t, 0]
        state = held_state[t] + jnp.sum(grad * grad, axis=0, keepdims=True) * (1.0 / width)
        made_state[t] = state
        made[t] = held[t, 1] - LEARN_RATE * grad / (jnp.sqrt(state) + ADA_EPS)
        new_row, new_state = results[t]
        for i, (src, dst) in enumerate(((made.at[t], new_row), (made_state.at[t], new_state))):
            store = pltpu.make_async_copy(src, dst, store_sem.at[t, i])
            store.start()
            stores.append(store)
    for store in stores:
        store.wait()


def body(
    left_rows, left_state, right_rows, right_state, relation,
    left_rows_wanted, right_rows_wanted,
    left_edge_position, right_edge_position, negative_position,
):
    rows, width = left_rows.shape
    edges = left_edge_position.shape[1]
    negs = negative_position.shape[1]
    owners = lax.axis_size("edge")
    chips = owners // 2
    both = edges + negs
    vmem = pl.BlockSpec(memory_space=pltpu.VMEM)
    hbm = pl.BlockSpec(memory_space=pl.ANY)
    dma = pltpu.SemaphoreType.DMA
    block = (width, rows)
    a_block = jax.ShapeDtypeStruct(block, F32)
    a_state = jax.ShapeDtypeStruct((1, rows), F32)
    left_t, right_t = left_rows.T, right_rows.T
    left_grad, right_grad, right_next, right_state_next = pl.pallas_call(
        round_kernel,
        out_shape=(a_block, a_block, a_block, a_state),
        in_specs=[hbm] * 9,
        out_specs=(vmem, vmem, hbm, hbm),
        scratch_shapes=[
            pltpu.VMEM(block, F32),
            pltpu.VMEM(block, F32),
            pltpu.VMEM((1, width), F32),
            pltpu.VMEM((owners, LANES), jnp.int32),
            pltpu.VMEM((owners, LANES), jnp.int32),
            pltpu.VMEM((1, edges), jnp.int32),
            pltpu.VMEM((1, edges), jnp.int32),
            pltpu.VMEM((1, negs), jnp.int32),
            pltpu.VMEM((2, chips, 2) + block, BF16),
            pltpu.VMEM((chips, 2, edges, rows), BF16),
            pltpu.VMEM((chips, 2, both, rows), BF16),
            pltpu.VMEM((1, edges), jnp.int32),
            pltpu.VMEM((1, both), jnp.int32),
            pltpu.VMEM((edges, LANES), jnp.int32),
            pltpu.VMEM((both, LANES), jnp.int32),
            pltpu.VMEM((width, edges), F32),
            pltpu.VMEM((width, both), F32),
            pltpu.VMEM((width, STRIP), F32),
            pltpu.VMEM((width, edges), BF16),
            pltpu.VMEM((edges, width), BF16),
            pltpu.VMEM((width, negs), BF16),
            pltpu.VMEM((edges, negs), BF16),
            pltpu.VMEM((1, edges), F32),
            pltpu.VMEM((width, edges), BF16),
            pltpu.VMEM((width, both), BF16),
            pltpu.VMEM((2, 2) + block, F32),
            pltpu.VMEM((2, 2, chips // 2) + block, BF16),
            pltpu.VMEM((2, 2, chips // 2) + block, BF16),
            pltpu.VMEM((2, chips) + block, BF16),
            pltpu.VMEM((2, chips) + block, BF16),
            pltpu.VMEM(block, BF16),
            pltpu.VMEM(block, BF16),
            dma((8,)),
            dma((2, 2, chips // 2, 2)), dma((2, 2, chips // 2, 2)), dma((2, chips, 2)), dma((2, chips, 2)),
            dma((2, 2, chips // 2)), dma((2, 2, chips // 2)), dma((2, chips)), dma((2, chips)),
            dma((3,)), dma((3,)),
        ],
        compiler_params=pltpu.CompilerParams(
            collective_id=0, has_side_effects=True, vmem_limit_bytes=62 * 1024 * 1024
        ),
        name="bucket_round",
    )(
        left_t, right_t, right_state.reshape(1, rows), relation.reshape(1, width),
        left_rows_wanted, right_rows_wanted, left_edge_position, right_edge_position, negative_position,
    )
    new_left, new_left_state, new_right, new_right_state = pl.pallas_call(
        update_kernel,
        out_shape=(a_block, a_state, a_block, a_state),
        in_specs=[hbm] * 6,
        out_specs=(hbm,) * 4,
        scratch_shapes=[
            pltpu.VMEM((2, 2) + block, F32), pltpu.VMEM((2,) + block, F32),
            pltpu.VMEM((2, 1, rows), F32), pltpu.VMEM((2, 1, rows), F32),
            dma((2, 3)), dma((2, 2)),
        ],
        name="adagrad",
    )(left_t, left_state.reshape(1, rows), left_grad, right_next, right_state_next, right_grad)
    return (new_left.T, new_left_state.reshape(rows), new_right.T, new_right_state.reshape(rows))


def solution(mesh):
    split = P(("dom", "edge"), None)
    return jax.shard_map(
        body,
        mesh=mesh,
        in_specs=(split, P(("dom", "edge")), split, P(("dom", "edge")), P(), split, split, split, split, split),
        out_specs=(split, P(("dom", "edge")), split, P(("dom", "edge"))),
        check_vma=False,
    )
```

```python
import jax
import jax.numpy as jnp
from jax import lax
from jax.experimental import pallas as pl
from jax.experimental.pallas import tpu as pltpu
from jax.sharding import PartitionSpec as P

LEARN_RATE = 0.1
ADA_EPS = 1e-10
MESH = pl.DeviceIdType.MESH
F32 = jnp.float32
BF16 = jnp.bfloat16

LEFT, RIGHT = 0, 1
HOPS = ((4, 3), (3, 4))
LANES = 128
STRIP = 256
CUT = 208


def round_kernel(
    left_hbm, left_state_hbm, right_hbm, right_state_hbm, relation_hbm,
    left_wanted_hbm, right_wanted_hbm, left_pos_hbm, right_pos_hbm, neg_pos_hbm,
    new_left_ref, new_left_state_ref, new_right_ref, new_right_state_ref,
    left_ref, left_state_ref, right_ref, right_state_ref, relation_ref, left_wanted_ref, right_wanted_ref,
    left_pos_ref, right_pos_ref, neg_pos_ref,
    tab,
    hot_left,
    hot_right,
    key_left,
    key_right,
    keyt_left,
    keyt_right,
    got_left,
    got_right,
    rel_col,
    query,
    query_rows,
    neg_t,
    push,
    pull,
    grad_left,
    grad_right,
    mine,
    ring_out,
    ring_in,
    pair_out,
    pair_in,
    own_out,
    own_in,
    rows_in,
    state_in,
    load_sem, ag_send, ag_recv, agp_send, agp_recv,
    rs_send, rs_recv, rsp_send, rsp_recv,
    misc_send, misc_recv,
):
    width, rows = left_ref.shape
    half = width // 2
    edges = left_pos_ref.shape[1]
    negs = neg_pos_ref.shape[1]
    doms = lax.axis_size("dom")
    owners = lax.axis_size("edge")
    chips = owners // 2
    far = chips // 2
    dom = lax.axis_index("dom")
    me = lax.axis_index("edge")
    z = me // 2
    core = lax.rem(me, 2)
    partner = z * 2 + (1 - core)
    ring = (lax.rem(me + 2, owners), lax.rem(me + owners - 2, owners))
    next_dom = lax.rem(dom + 1, doms)
    prev_dom = lax.rem(dom + doms - 1, doms)

    barrier = pltpu.get_barrier_semaphore()
    for d, e in (
        (dom, partner), (dom, ring[0]), (dom, ring[1]),
        (prev_dom, me), (prev_dom, ring[0]), (prev_dom, ring[1]),
    ):
        pl.semaphore_signal(barrier, inc=1, device_id=(d, e), device_id_type=MESH)

    loads = [
        pltpu.make_async_copy(src, dst, load_sem.at[i])
        for i, (src, dst) in enumerate((
            (left_hbm, left_ref), (right_hbm, right_ref), (relation_hbm, relation_ref),
            (left_state_hbm, left_state_ref), (right_state_hbm, right_state_ref),
            (left_wanted_hbm, left_wanted_ref), (right_wanted_hbm, right_wanted_ref),
            (left_pos_hbm, left_pos_ref), (right_pos_hbm, right_pos_ref), (neg_pos_hbm, neg_pos_ref),
        ))
    ]
    for load in loads:
        load.start()
    loads[0].wait()
    tab[LEFT, z, core] = left_ref[...].astype(BF16)
    pl.semaphore_wait(barrier, 6)

    started = []

    def send(src, dst, send_sem, recv_sem, d, e):
        copy = pltpu.make_async_remote_copy(
            src_ref=src, dst_ref=dst, send_sem=send_sem, recv_sem=recv_sem,
            device_id=(d, e), device_id_type=MESH,
        )
        copy.start()
        started.append(copy)
        return copy

    def at_chip(offset):
        return lax.rem(z + offset + 2 * chips, chips)

    PARTS = (pl.ds(0, CUT), pl.ds(CUT, width - CUT))
    ring_copy = {}
    pair_copy = {}

    def piece(t, offset, part):
        block = tab.at[t, at_chip(offset), core]
        return block if part is None else block.at[PARTS[part]]

    def ring_gather(t, way, step, part=None):
        block = piece(t, -(step - 1) if way == 0 else step - 1, part)
        sem = (t, way, step - 1, part or 0)
        ring_copy[t, way, step, part] = send(block, block, ag_send.at[sem], ag_recv.at[sem], dom, ring[way])

    def pair_gather(t, offset, part=None):
        block = piece(t, offset, part)
        sem = (t, offset % chips, part or 0)
        copy = send(block, block, agp_send.at[sem], agp_recv.at[sem], dom, partner)
        pair_copy.setdefault((t, offset % chips), []).append(copy)

    def arrive(t, step, turn=None):
        parts = [None if turn is None else (way + turn) % 2 for way in (0, 1)]
        for way in (0, 1):
            ring_copy[t, way, step, parts[way]].wait_recv()
            if step < far - 1:
                ring_gather(t, way, step + 1, parts[way])
            elif step == far - 1 and parts[way] in (None, way):
                ring_gather(t, way, far, way)
        for way in (0, 1):
            pair_gather(t, -step if way == 0 else step, parts[way])

    def from_pair(t, offset):
        for copy in pair_copy[t, offset % chips]:
            copy.wait_recv()

    for way in (0, 1):
        ring_gather(LEFT, way, 1)
    pair_gather(LEFT, 0)
    for load in loads[1:]:
        load.wait()
    tab[RIGHT, z, core] = right_ref[...].astype(BF16)

    def place(pos, wanted_ref):
        count = pos.shape[1]
        col = lax.broadcasted_iota(jnp.int32, (LANES, count), 0)
        hot = jnp.where(col == lax.rem(pos, LANES), 1.0, 0.0).astype(BF16)
        by_owner = jnp.dot(wanted_ref[...].astype(F32).astype(BF16), hot, preferred_element_type=F32)
        owner = pos // LANES
        own = lax.broadcasted_iota(jnp.int32, (owners, count), 0)
        row = jnp.sum(jnp.where(own == owner, by_owner, 0.0), axis=0, keepdims=True)
        return owner.astype(F32) * float(rows) + row

    def fill_keys(key, start, count, keyt, key_ref):
        key_ref[:, pl.ds(start, count)] = key.astype(jnp.int32)
        keyt[pl.ds(start, count), :] = jnp.transpose(jnp.broadcast_to(key, (LANES, count))).astype(jnp.int32)

    fill_keys(place(left_pos_ref[...], left_wanted_ref), 0, edges, keyt_left, key_left)
    fill_keys(place(right_pos_ref[...], right_wanted_ref), 0, edges, keyt_right, key_right)
    fill_keys(place(neg_pos_ref[...], right_wanted_ref), edges, negs, keyt_right, key_right)

    for way in (0, 1):
        ring_gather(RIGHT, way, 1, way)
    pair_gather(RIGHT, 0)
    rows_copy = send(right_ref, rows_in, misc_send.at[0], misc_recv.at[0], next_dom, me)
    state_copy = send(right_state_ref, state_in, misc_send.at[1], misc_recv.at[1], next_dom, me)

    row_at = lax.broadcasted_iota(jnp.int32, (width, width), 0)
    col_at = lax.broadcasted_iota(jnp.int32, (width, width), 1)
    col = jnp.sum(jnp.where(row_at == col_at, relation_ref[...], 0.0), axis=1, keepdims=True)
    rel_col[...] = jnp.broadcast_to(col, (width, STRIP))

    def fill_hot(hot, keyt, chip):
        count = keyt.shape[0]

        def step(i, _):
            at = pl.ds(pl.multiple_of(i * 256, 256), 256)
            lane = lax.broadcasted_iota(jnp.int32, (256, LANES), 1)
            for c in (0, 1):
                local = keyt[at, :] - (chip * 2 + c) * rows
                for h in range(rows // LANES):
                    hot[chip, c, at, pl.ds(h * LANES, LANES)] = jnp.where(
                        lane + h * LANES == local, 1.0, 0.0
                    ).astype(BF16)
            return 0

        lax.fori_loop(0, count // 256, step, 0)

    def fill(*some):
        for chip in some:
            fill_hot(hot_left, keyt_left, chip)
            fill_hot(hot_right, keyt_right, chip)

    TILE = 512

    def take(t, offsets, first=False):
        key_ref, got = ((key_left, got_left), (key_right, got_right))[t]
        count = key_ref.shape[1]
        for offset in offsets:
            from_pair(t, offset)

        def step(i, _):
            at = pl.ds(pl.multiple_of(i * TILE, TILE), TILE)
            row = lax.broadcasted_iota(jnp.int32, (rows, TILE), 0)
            part = None
            for offset in offsets:
                chip = at_chip(offset)
                for c in (0, 1):
                    local = key_ref[:, at] - (chip * 2 + c) * rows
                    hot = jnp.where(row == local, 1.0, 0.0).astype(BF16)
                    term = jnp.dot(tab[t, chip, c], hot, preferred_element_type=F32)
                    part = term if part is None else part + term
            if first:
                got[:, at] = part
            else:
                got[:, at] += part
            return 0

        lax.fori_loop(0, count // TILE, step, 0)

    fill(0, 1, 2, 3)
    arrive(LEFT, 1)
    for way in (0, 1):
        ring_gather(RIGHT, way, 1, 1 - way)
    take(LEFT, (0,), first=True)
    take(RIGHT, (0,), first=True)
    fill(4, 5, 6, 7)
    arrive(LEFT, 2)
    arrive(RIGHT, 1, 0)
    take(LEFT, (-1, 1))
    take(LEFT, (-2, 2))
    arrive(LEFT, 3)
    arrive(RIGHT, 1, 1)
    take(RIGHT, (-1, 1))
    arrive(RIGHT, 2, 0)
    take(LEFT, (-3, 3))
    arrive(LEFT, far, 0)
    arrive(RIGHT, 2, 1)
    take(LEFT, (far,))

    def strip(i):
        return pl.ds(pl.multiple_of(i * STRIP, STRIP), STRIP)

    def make_query(i, _):
        at = strip(i)
        pr = rel_col[:half, :]
        pi = rel_col[half:, :]
        lr = got_left[:half, at]
        li = got_left[half:, at]
        q = jnp.concatenate([lr * pr - li * pi, lr * pi + li * pr], axis=0)
        query[:, at] = q.astype(BF16)
        query_rows[at, :] = jnp.transpose(q).astype(BF16)
        return 0

    lax.fori_loop(0, edges // STRIP, make_query, 0)
    arrive(RIGHT, 3, 0)
    take(RIGHT, (-2, 2))
    arrive(RIGHT, 3, 1)
    take(RIGHT, (-3, 3))
    arrive(RIGHT, far, 0)

    def last_columns(at, cores):
        chip = at_chip(far)
        row = lax.broadcasted_iota(jnp.int32, (rows, at.size), 0)
        part = got_right[:, at]
        for c in cores:
            local = key_right[:, at] - (chip * 2 + c) * rows
            hot = jnp.where(row == local, 1.0, 0.0).astype(BF16)
            part = part + jnp.dot(tab[RIGHT, chip, c], hot, preferred_element_type=F32)
        got_right[:, at] = part
        return part

    neg_cols = pl.ds(edges, negs)
    last_columns(neg_cols, (core,))
    for i in range(edges // STRIP):
        last_columns(pl.ds(i * STRIP, STRIP), (core,))
    from_pair(RIGHT, far)
    neg_t[...] = last_columns(neg_cols, (1 - core,)).astype(BF16)

    neg_total = None
    for i in range(edges // STRIP):
        at = pl.ds(i * STRIP, STRIP)
        negative = jnp.dot(query_rows[at, :], neg_t[...], preferred_element_type=F32)
        p = (jnp.tanh(negative * 0.5) * (0.5 / negs) + (0.5 / negs)).astype(BF16)
        push[at, :] = p
        term = jnp.dot(query[:, at], p, preferred_element_type=F32)
        neg_total = term if neg_total is None else neg_total + term
        q = query[:, at].astype(F32)
        positive = jnp.sum(q * last_columns(at, (1 - core,)), axis=0, keepdims=True)
        weight = -jax.nn.sigmoid(-positive)
        pull[:, at] = weight
        grad_right[:, at] = (weight * q).astype(BF16)
    grad_right[:, neg_cols] = neg_total.astype(BF16)

    def left_grads(*strips):
        pr = rel_col[:half, :]
        pi = rel_col[half:, :]
        for i in strips:
            at = pl.ds(i * STRIP, STRIP)
            g = pull[:, at] * got_right[:, at] + lax.dot_general(
                neg_t[...], push[at, :], (((1,), (1,)), ((), ())), preferred_element_type=F32
            )
            gr = g[:half, :]
            gi = g[half:, :]
            grad_left[:, at] = jnp.concatenate([gr * pr + gi * pi, gi * pr - gr * pi], axis=0).astype(BF16)

    def dense(t, offset, c):
        grad, hot = ((grad_left, hot_left), (grad_right, hot_right))[t]
        return jnp.dot(grad[...], hot[at_chip(offset), c], preferred_element_type=F32)

    def give(t, offset):
        slot = offset % chips
        pair_out[t, slot] = dense(t, offset, 1 - core).astype(BF16)
        pair_copy[t, slot] = send(
            pair_out.at[t, slot], pair_in.at[t, slot], rsp_send.at[t, slot], rsp_recv.at[t, slot], dom, partner
        )

    def with_pair(t, offset, part):
        slot = offset % chips
        pair_copy[t, slot].wait_recv()
        return part + pair_in[t, slot].astype(F32)

    rs_copy = {}

    def pass_on(t, way, step):
        sem = (t, way, step - 1)
        out, into = ring_out.at[sem], ring_in.at[sem]
        if step == 1:
            out, into = out.at[PARTS[way]], into.at[PARTS[way]]
        last = t == RIGHT and step == far
        rs_copy[sem] = send(out, into, rs_send.at[sem], rs_recv.at[sem], next_dom if last else dom, ring[way])

    def came(t, way, step, part=slice(None)):
        return ring_in[t, way, step - 1, part].astype(F32)

    def first(t):
        for way in (0, 1):
            part = PARTS[way]
            ring_out[t, way, 0, part] = (
                mine[t, 0, part] + pair_in[t, far, part].astype(F32)
            ).astype(BF16)
            pass_on(t, way, 1)

    def ready(t, step):
        offsets = (far + 1 - step, step - far - 1)
        for offset in offsets:
            give(t, offset)
        parts = [dense(t, offset, core) for offset in offsets]
        for way in (0, 1):
            mine[t, way] = with_pair(t, offsets[way], parts[way])

    def onward(t, step):
        for way in (0, 1):
            rs_copy[t, way, step - 2].wait_recv()
            if step == 2:
                part, other = PARTS[way], PARTS[1 - way]
                ring_out[t, way, 1, part] = (mine[t, way, part] + came(t, way, 1, part)).astype(BF16)
                ring_out[t, way, 1, other] = mine[t, way, other].astype(BF16)
            else:
                ring_out[t, way, step - 1] = (mine[t, way] + came(t, way, step - 1)).astype(BF16)
            pass_on(t, way, step)

    def finish(t, row, state, total):
        for way in (0, 1):
            rs_copy[t, way, far - 1].wait_recv()
            total = total + came(t, way, far)
        state = state + jnp.sum(total * total, axis=0, keepdims=True) * (1.0 / width)
        (new_left_state_ref, new_right_state_ref)[t][...] = state
        (new_left_ref, new_right_ref)[t][...] = row - LEARN_RATE * total / (jnp.sqrt(state) + ADA_EPS)

    strips = range(edges // STRIP)
    give(RIGHT, far)
    mine[RIGHT, 0] = dense(RIGHT, far, core)
    left_grads(*strips[:-1])
    pair_copy[RIGHT, far].wait_recv()
    first(RIGHT)
    left_grads(*strips[-1:])
    give(LEFT, far)
    mine[LEFT, 0] = dense(LEFT, far, core)
    ready_right = (far - 1, 1 - far)
    for offset in ready_right:
        give(RIGHT, offset)
    pair_copy[LEFT, far].wait_recv()
    first(LEFT)
    for way in (0, 1):
        mine[RIGHT, way] = with_pair(RIGHT, ready_right[way], dense(RIGHT, ready_right[way], core))
    onward(RIGHT, 2)
    ready(LEFT, 2)
    give(RIGHT, 0)
    onward(LEFT, 2)
    own_out[...] = with_pair(RIGHT, 0, dense(RIGHT, 0, core)).astype(BF16)
    own_copy = send(own_out, own_in, misc_send.at[2], misc_recv.at[2], next_dom, me)
    ready(RIGHT, 3)
    onward(RIGHT, 3)
    ready(LEFT, 3)
    onward(LEFT, 3)
    ready(RIGHT, 4)
    onward(RIGHT, 4)
    ready(LEFT, 4)
    onward(LEFT, 4)
    give(LEFT, 0)
    mine[LEFT, 2] = with_pair(LEFT, 0, dense(LEFT, 0, core))
    rows_copy.wait_recv()
    state_copy.wait_recv()
    own_copy.wait_recv()
    finish(RIGHT, rows_in[...], state_in[...], own_in[...].astype(F32))
    finish(LEFT, left_ref[...], left_state_ref[...], mine[LEFT, 2])
    for copy in started:
        copy.wait_send()


def place_kernel(*refs):
    sems = refs[-1]
    copies = [pltpu.make_async_copy(refs[i], refs[4 + i], sems.at[i]) for i in range(4)]
    for copy in copies:
        copy.start()
    for copy in copies:
        copy.wait()


def body(
    left_rows, left_state, right_rows, right_state, relation,
    left_rows_wanted, right_rows_wanted,
    left_edge_position, right_edge_position, negative_position,
):
    rows, width = left_rows.shape
    edges = left_edge_position.shape[1]
    negs = negative_position.shape[1]
    owners = lax.axis_size("edge")
    chips = owners // 2
    both = edges + negs
    hbm = pl.BlockSpec(memory_space=pl.ANY)
    vmem = pl.BlockSpec(memory_space=pltpu.VMEM)
    dma = pltpu.SemaphoreType.DMA
    block = (width, rows)
    a_block = jax.ShapeDtypeStruct(block, F32)
    a_state = jax.ShapeDtypeStruct((1, rows), F32)
    made = pl.pallas_call(
        round_kernel,
        out_shape=(pltpu.VMEM(block, F32), pltpu.VMEM((1, rows), F32), pltpu.VMEM(block, F32), pltpu.VMEM((1, rows), F32)),
        in_specs=[hbm] * 10,
        out_specs=(vmem,) * 4,
        scratch_shapes=[
            pltpu.VMEM(block, F32),
            pltpu.VMEM((1, rows), F32),
            pltpu.VMEM(block, F32),
            pltpu.VMEM((1, rows), F32),
            pltpu.VMEM((1, width), F32),
            pltpu.VMEM((owners, LANES), jnp.int32),
            pltpu.VMEM((owners, LANES), jnp.int32),
            pltpu.VMEM((1, edges), jnp.int32),
            pltpu.VMEM((1, edges), jnp.int32),
            pltpu.VMEM((1, negs), jnp.int32),
            pltpu.VMEM((2, chips, 2) + block, BF16),
            pltpu.VMEM((chips, 2, edges, rows), BF16),
            pltpu.VMEM((chips, 2, both, rows), BF16),
            pltpu.VMEM((1, edges), jnp.int32),
            pltpu.VMEM((1, both), jnp.int32),
            pltpu.VMEM((edges, LANES), jnp.int32),
            pltpu.VMEM((both, LANES), jnp.int32),
            pltpu.VMEM((width, edges), F32),
            pltpu.VMEM((width, both), F32),
            pltpu.VMEM((width, STRIP), F32),
            pltpu.VMEM((width, edges), BF16),
            pltpu.VMEM((edges, width), BF16),
            pltpu.VMEM((width, negs), BF16),
            pltpu.VMEM((edges, negs), BF16),
            pltpu.VMEM((1, edges), F32),
            pltpu.VMEM((width, edges), BF16),
            pltpu.VMEM((width, both), BF16),
            pltpu.VMEM((2, 3) + block, F32),
            pltpu.VMEM((2, 2, chips // 2) + block, BF16),
            pltpu.VMEM((2, 2, chips // 2) + block, BF16),
            pltpu.VMEM((2, chips) + block, BF16),
            pltpu.VMEM((2, chips) + block, BF16),
            pltpu.VMEM(block, BF16),
            pltpu.VMEM(block, BF16),
            pltpu.VMEM(block, F32),
            pltpu.VMEM((1, rows), F32),
            dma((10,)),
            dma((2, 2, chips // 2, 2)), dma((2, 2, chips // 2, 2)), dma((2, chips, 2)), dma((2, chips, 2)),
            dma((2, 2, chips // 2)), dma((2, 2, chips // 2)), dma((2, chips)), dma((2, chips)),
            dma((3,)), dma((3,)),
        ],
        compiler_params=pltpu.CompilerParams(
            collective_id=0, has_side_effects=True, vmem_limit_bytes=58 * 1024 * 1024
        ),
        name="bucket_round",
    )(
        left_rows.T, left_state.reshape(1, rows), right_rows.T, right_state.reshape(1, rows),
        relation.reshape(1, width), left_rows_wanted, right_rows_wanted,
        left_edge_position, right_edge_position, negative_position,
    )
    new_left, new_left_state, new_right, new_right_state = pl.pallas_call(
        place_kernel,
        out_shape=(a_block, a_state, a_block, a_state),
        in_specs=[vmem] * 4,
        out_specs=(hbm,) * 4,
        scratch_shapes=[dma((4,))],
        name="place",
    )(*(pltpu.with_memory_space_constraint(x, pltpu.VMEM) for x in made))
    return (new_left.T, new_left_state.reshape(rows), new_right.T, new_right_state.reshape(rows))


def solution(mesh):
    split = P(("dom", "edge"), None)
    return jax.shard_map(
        body,
        mesh=mesh,
        in_specs=(split, P(("dom", "edge")), split, P(("dom", "edge")), P(), split, split, split, split, split),
        out_specs=(split, P(("dom", "edge")), split, P(("dom", "edge"))),
        check_vma=False,
    )
```

```python
import jax
import jax.numpy as jnp
from jax import lax
from jax.experimental import pallas as pl
from jax.experimental.pallas import tpu as pltpu
from jax.sharding import PartitionSpec as P

LEARN_RATE = 0.1
ADA_EPS = 1e-10
MESH = pl.DeviceIdType.MESH
F32 = jnp.float32
BF16 = jnp.bfloat16

LEFT, RIGHT = 0, 1
HOPS = ((4, 3), (3, 4))
LANES = 128
STRIP = 256
CUT = 208


def round_kernel(
    left_hbm, left_state_hbm, right_hbm, right_state_hbm, relation_hbm,
    left_wanted_hbm, right_wanted_hbm, left_pos_hbm, right_pos_hbm, neg_pos_hbm,
    new_left_ref, new_left_state_ref, new_right_ref, new_right_state_ref,
    left_ref, left_state_ref, right_ref, right_state_ref, relation_ref, left_wanted_ref, right_wanted_ref,
    left_pos_ref, right_pos_ref, neg_pos_ref,
    tab,
    hot_left,
    hot_right,
    key_left,
    key_right,
    keyt_left,
    keyt_right,
    got_left,
    got_right,
    rel_col,
    query,
    query_rows,
    neg_t,
    push,
    pull,
    grad_left,
    grad_right,
    mine,
    ring_out,
    ring_in,
    pair_out,
    pair_in,
    own_out,
    own_in,
    rows_in,
    state_in,
    load_sem, ag_send, ag_recv, agp_send, agp_recv,
    rs_send, rs_recv, rsp_send, rsp_recv,
    misc_send, misc_recv,
):
    width, rows = left_ref.shape
    half = width // 2
    edges = left_pos_ref.shape[1]
    negs = neg_pos_ref.shape[1]
    doms = lax.axis_size("dom")
    owners = lax.axis_size("edge")
    chips = owners // 2
    far = chips // 2
    dom = lax.axis_index("dom")
    me = lax.axis_index("edge")
    z = me // 2
    core = lax.rem(me, 2)
    partner = z * 2 + (1 - core)
    ring = (lax.rem(me + 2, owners), lax.rem(me + owners - 2, owners))
    next_dom = lax.rem(dom + 1, doms)
    prev_dom = lax.rem(dom + doms - 1, doms)

    barrier = pltpu.get_barrier_semaphore()
    for d, e in (
        (dom, partner), (dom, ring[0]), (dom, ring[1]),
        (prev_dom, me), (prev_dom, ring[0]), (prev_dom, ring[1]),
    ):
        pl.semaphore_signal(barrier, inc=1, device_id=(d, e), device_id_type=MESH)

    loads = [
        pltpu.make_async_copy(src, dst, load_sem.at[i])
        for i, (src, dst) in enumerate((
            (left_hbm, left_ref), (right_hbm, right_ref), (relation_hbm, relation_ref),
            (left_state_hbm, left_state_ref), (right_state_hbm, right_state_ref),
            (left_wanted_hbm, left_wanted_ref), (right_wanted_hbm, right_wanted_ref),
            (left_pos_hbm, left_pos_ref), (right_pos_hbm, right_pos_ref), (neg_pos_hbm, neg_pos_ref),
        ))
    ]
    for load in loads:
        load.start()
    loads[0].wait()
    tab[LEFT, z, core] = left_ref[...].astype(BF16)
    pl.semaphore_wait(barrier, 6)

    started = []

    def send(src, dst, send_sem, recv_sem, d, e):
        copy = pltpu.make_async_remote_copy(
            src_ref=src, dst_ref=dst, send_sem=send_sem, recv_sem=recv_sem,
            device_id=(d, e), device_id_type=MESH,
        )
        copy.start()
        started.append(copy)
        return copy

    def at_chip(offset):
        return lax.rem(z + offset + 2 * chips, chips)

    PARTS = (pl.ds(0, CUT), pl.ds(CUT, width - CUT))
    ring_copy = {}
    pair_copy = {}

    def piece(t, offset, part):
        block = tab.at[t, at_chip(offset), core]
        return block if part is None else block.at[PARTS[part]]

    def ring_gather(t, way, step, part=None):
        block = piece(t, -(step - 1) if way == 0 else step - 1, part)
        sem = (t, way, step - 1, part or 0)
        ring_copy[t, way, step, part] = send(block, block, ag_send.at[sem], ag_recv.at[sem], dom, ring[way])

    def pair_gather(t, offset, part=None):
        block = piece(t, offset, part)
        sem = (t, offset % chips, part or 0)
        copy = send(block, block, agp_send.at[sem], agp_recv.at[sem], dom, partner)
        pair_copy.setdefault((t, offset % chips), []).append(copy)

    def arrive(t, step, turn=None):
        parts = [None if turn is None else (way + turn) % 2 for way in (0, 1)]
        for way in (0, 1):
            ring_copy[t, way, step, parts[way]].wait_recv()
            if step < far - 1:
                ring_gather(t, way, step + 1, parts[way])
            elif step == far - 1 and parts[way] in (None, way):
                ring_gather(t, way, far, way)
        for way in (0, 1):
            pair_gather(t, -step if way == 0 else step, parts[way])

    def from_pair(t, offset):
        for copy in pair_copy[t, offset % chips]:
            copy.wait_recv()

    for way in (0, 1):
        ring_gather(LEFT, way, 1)
    pair_gather(LEFT, 0)
    for load in loads[1:]:
        load.wait()
    tab[RIGHT, z, core] = right_ref[...].astype(BF16)

    def place(pos, wanted_ref):
        count = pos.shape[1]
        col = lax.broadcasted_iota(jnp.int32, (LANES, count), 0)
        hot = jnp.where(col == lax.rem(pos, LANES), 1.0, 0.0).astype(BF16)
        by_owner = jnp.dot(wanted_ref[...].astype(F32).astype(BF16), hot, preferred_element_type=F32)
        owner = pos // LANES
        own = lax.broadcasted_iota(jnp.int32, (owners, count), 0)
        row = jnp.sum(jnp.where(own == owner, by_owner, 0.0), axis=0, keepdims=True)
        return owner.astype(F32) * float(rows) + row

    def fill_keys(key, start, count, keyt, key_ref):
        key_ref[:, pl.ds(start, count)] = key.astype(jnp.int32)
        keyt[pl.ds(start, count), :] = jnp.transpose(jnp.broadcast_to(key, (LANES, count))).astype(jnp.int32)

    fill_keys(place(left_pos_ref[...], left_wanted_ref), 0, edges, keyt_left, key_left)
    fill_keys(place(right_pos_ref[...], right_wanted_ref), 0, edges, keyt_right, key_right)
    fill_keys(place(neg_pos_ref[...], right_wanted_ref), edges, negs, keyt_right, key_right)

    for way in (0, 1):
        ring_gather(RIGHT, way, 1, way)
    pair_gather(RIGHT, 0)
    rows_copy = send(right_ref, rows_in, misc_send.at[0], misc_recv.at[0], next_dom, me)
    state_copy = send(right_state_ref, state_in, misc_send.at[1], misc_recv.at[1], next_dom, me)

    row_at = lax.broadcasted_iota(jnp.int32, (width, width), 0)
    col_at = lax.broadcasted_iota(jnp.int32, (width, width), 1)
    col = jnp.sum(jnp.where(row_at == col_at, relation_ref[...], 0.0), axis=1, keepdims=True)
    rel_col[...] = jnp.broadcast_to(col, (width, STRIP))

    def fill_hot(hot, keyt, chip):
        count = keyt.shape[0]

        def step(i, _):
            at = pl.ds(pl.multiple_of(i * 256, 256), 256)
            lane = lax.broadcasted_iota(jnp.int32, (256, LANES), 1)
            for c in (0, 1):
                local = keyt[at, :] - (chip * 2 + c) * rows
                for h in range(rows // LANES):
                    hot[chip, c, at, pl.ds(h * LANES, LANES)] = jnp.where(
                        lane + h * LANES == local, 1.0, 0.0
                    ).astype(BF16)
            return 0

        lax.fori_loop(0, count // 256, step, 0)

    def fill(*some):
        for chip in some:
            fill_hot(hot_left, keyt_left, chip)
            fill_hot(hot_right, keyt_right, chip)

    TILE = 512

    def take(t, offsets, first=False):
        key_ref, got = ((key_left, got_left), (key_right, got_right))[t]
        count = key_ref.shape[1]
        for offset in offsets:
            from_pair(t, offset)

        def step(i, _):
            at = pl.ds(pl.multiple_of(i * TILE, TILE), TILE)
            row = lax.broadcasted_iota(jnp.int32, (rows, TILE), 0)
            part = None
            for offset in offsets:
                chip = at_chip(offset)
                for c in (0, 1):
                    local = key_ref[:, at] - (chip * 2 + c) * rows
                    hot = jnp.where(row == local, 1.0, 0.0).astype(BF16)
                    term = jnp.dot(tab[t, chip, c], hot, preferred_element_type=F32)
                    part = term if part is None else part + term
            if first:
                got[:, at] = part
            else:
                got[:, at] += part
            return 0

        lax.fori_loop(0, count // TILE, step, 0, unroll=True)

    fill(0, 1, 2, 3)
    arrive(LEFT, 1)
    for way in (0, 1):
        ring_gather(RIGHT, way, 1, 1 - way)
    take(LEFT, (0,), first=True)
    take(RIGHT, (0,), first=True)
    fill(4, 5, 6, 7)
    arrive(LEFT, 2)
    arrive(RIGHT, 1, 0)
    take(LEFT, (-1, 1))
    take(LEFT, (-2, 2))
    arrive(LEFT, 3)
    arrive(RIGHT, 1, 1)
    take(RIGHT, (-1, 1))
    arrive(RIGHT, 2, 0)
    take(LEFT, (-3, 3))
    arrive(LEFT, far, 0)
    arrive(RIGHT, 2, 1)
    take(LEFT, (far,))

    def strip(i):
        return pl.ds(pl.multiple_of(i * STRIP, STRIP), STRIP)

    def make_query(i, _):
        at = strip(i)
        pr = rel_col[:half, :]
        pi = rel_col[half:, :]
        lr = got_left[:half, at]
        li = got_left[half:, at]
        q = jnp.concatenate([lr * pr - li * pi, lr * pi + li * pr], axis=0)
        query[:, at] = q.astype(BF16)
        query_rows[at, :] = jnp.transpose(q).astype(BF16)
        return 0

    lax.fori_loop(0, edges // STRIP, make_query, 0, unroll=True)
    arrive(RIGHT, 3, 0)
    take(RIGHT, (-2, 2))
    arrive(RIGHT, 3, 1)
    take(RIGHT, (-3, 3))
    arrive(RIGHT, far, 0)

    def last_columns(at, cores):
        chip = at_chip(far)
        row = lax.broadcasted_iota(jnp.int32, (rows, at.size), 0)
        part = got_right[:, at]
        for c in cores:
            local = key_right[:, at] - (chip * 2 + c) * rows
            hot = jnp.where(row == local, 1.0, 0.0).astype(BF16)
            part = part + jnp.dot(tab[RIGHT, chip, c], hot, preferred_element_type=F32)
        got_right[:, at] = part
        return part

    neg_cols = pl.ds(edges, negs)
    last_columns(neg_cols, (core,))
    for i in range(edges // STRIP):
        last_columns(pl.ds(i * STRIP, STRIP), (core,))
    from_pair(RIGHT, far)
    neg_t[...] = last_columns(neg_cols, (1 - core,)).astype(BF16)

    strips = range(edges // STRIP)
    for i in strips:
        at = pl.ds(i * STRIP, STRIP)
        negative = jnp.dot(query_rows[at, :], neg_t[...], preferred_element_type=F32)
        push[at, :] = (jnp.tanh(negative * 0.5) * (0.5 / negs) + (0.5 / negs)).astype(BF16)
        q = query[:, at].astype(F32)
        positive = jnp.sum(q * last_columns(at, (1 - core,)), axis=0, keepdims=True)
        weight = -jax.nn.sigmoid(-positive)
        pull[:, at] = weight
        grad_right[:, at] = (weight * q).astype(BF16)
    grad_right[:, neg_cols] = jnp.dot(query[...], push[...], preferred_element_type=F32).astype(BF16)

    def left_grads(*strips):
        pr = rel_col[:half, :]
        pi = rel_col[half:, :]
        for i in strips:
            at = pl.ds(i * STRIP, STRIP)
            g = pull[:, at] * got_right[:, at] + lax.dot_general(
                neg_t[...], push[at, :], (((1,), (1,)), ((), ())), preferred_element_type=F32
            )
            gr = g[:half, :]
            gi = g[half:, :]
            grad_left[:, at] = jnp.concatenate([gr * pr + gi * pi, gi * pr - gr * pi], axis=0).astype(BF16)

    def dense(t, offset, c):
        grad, hot = ((grad_left, hot_left), (grad_right, hot_right))[t]
        return jnp.dot(grad[...], hot[at_chip(offset), c], preferred_element_type=F32)

    def give(t, offset):
        slot = offset % chips
        pair_out[t, slot] = dense(t, offset, 1 - core).astype(BF16)
        pair_copy[t, slot] = send(
            pair_out.at[t, slot], pair_in.at[t, slot], rsp_send.at[t, slot], rsp_recv.at[t, slot], dom, partner
        )

    def with_pair(t, offset, part):
        slot = offset % chips
        pair_copy[t, slot].wait_recv()
        return part + pair_in[t, slot].astype(F32)

    rs_copy = {}

    def pass_on(t, way, step):
        sem = (t, way, step - 1)
        out, into = ring_out.at[sem], ring_in.at[sem]
        if step == 1:
            out, into = out.at[PARTS[way]], into.at[PARTS[way]]
        last = t == RIGHT and step == far
        rs_copy[sem] = send(out, into, rs_send.at[sem], rs_recv.at[sem], next_dom if last else dom, ring[way])

    def came(t, way, step, part=slice(None)):
        return ring_in[t, way, step - 1, part].astype(F32)

    def first(t):
        for way in (0, 1):
            part = PARTS[way]
            ring_out[t, way, 0, part] = (
                mine[t, 0, part] + pair_in[t, far, part].astype(F32)
            ).astype(BF16)
            pass_on(t, way, 1)

    def ready(t, step):
        offsets = (far + 1 - step, step - far - 1)
        for offset in offsets:
            give(t, offset)
        parts = [dense(t, offset, core) for offset in offsets]
        for way in (0, 1):
            mine[t, way] = with_pair(t, offsets[way], parts[way])

    def onward(t, step):
        for way in (0, 1):
            rs_copy[t, way, step - 2].wait_recv()
            if step == 2:
                part, other = PARTS[way], PARTS[1 - way]
                ring_out[t, way, 1, part] = (mine[t, way, part] + came(t, way, 1, part)).astype(BF16)
                ring_out[t, way, 1, other] = mine[t, way, other].astype(BF16)
            else:
                ring_out[t, way, step - 1] = (mine[t, way] + came(t, way, step - 1)).astype(BF16)
            pass_on(t, way, step)

    def finish(t, row, state, total):
        for way in (0, 1):
            rs_copy[t, way, far - 1].wait_recv()
            total = total + came(t, way, far)
        state = state + jnp.sum(total * total, axis=0, keepdims=True) * (1.0 / width)
        (new_left_state_ref, new_right_state_ref)[t][...] = state
        (new_left_ref, new_right_ref)[t][...] = row - LEARN_RATE * total / (jnp.sqrt(state) + ADA_EPS)

    give(RIGHT, far)
    mine[RIGHT, 0] = dense(RIGHT, far, core)
    left_grads(*strips[:-1])
    pair_copy[RIGHT, far].wait_recv()
    first(RIGHT)
    left_grads(*strips[-1:])
    give(LEFT, far)
    mine[LEFT, 0] = dense(LEFT, far, core)
    ready_right = (far - 1, 1 - far)
    for offset in ready_right:
        give(RIGHT, offset)
    pair_copy[LEFT, far].wait_recv()
    first(LEFT)
    for way in (0, 1):
        mine[RIGHT, way] = with_pair(RIGHT, ready_right[way], dense(RIGHT, ready_right[way], core))
    onward(RIGHT, 2)
    ready(LEFT, 2)
    give(RIGHT, 0)
    onward(LEFT, 2)
    own_out[...] = with_pair(RIGHT, 0, dense(RIGHT, 0, core)).astype(BF16)
    own_copy = send(own_out, own_in, misc_send.at[2], misc_recv.at[2], next_dom, me)
    ready(RIGHT, 3)
    onward(RIGHT, 3)
    ready(LEFT, 3)
    onward(LEFT, 3)
    ready(RIGHT, 4)
    onward(RIGHT, 4)
    ready(LEFT, 4)
    onward(LEFT, 4)
    give(LEFT, 0)
    mine[LEFT, 2] = with_pair(LEFT, 0, dense(LEFT, 0, core))
    rows_copy.wait_recv()
    state_copy.wait_recv()
    own_copy.wait_recv()
    finish(RIGHT, rows_in[...], state_in[...], own_in[...].astype(F32))
    finish(LEFT, left_ref[...], left_state_ref[...], mine[LEFT, 2])
    for copy in started:
        copy.wait_send()


def place_kernel(*refs):
    sems = refs[-1]
    copies = [pltpu.make_async_copy(refs[i], refs[4 + i], sems.at[i]) for i in range(4)]
    for copy in copies:
        copy.start()
    for copy in copies:
        copy.wait()


def body(
    left_rows, left_state, right_rows, right_state, relation,
    left_rows_wanted, right_rows_wanted,
    left_edge_position, right_edge_position, negative_position,
):
    rows, width = left_rows.shape
    edges = left_edge_position.shape[1]
    negs = negative_position.shape[1]
    owners = lax.axis_size("edge")
    chips = owners // 2
    both = edges + negs
    hbm = pl.BlockSpec(memory_space=pl.ANY)
    vmem = pl.BlockSpec(memory_space=pltpu.VMEM)
    dma = pltpu.SemaphoreType.DMA
    block = (width, rows)
    a_block = jax.ShapeDtypeStruct(block, F32)
    a_state = jax.ShapeDtypeStruct((1, rows), F32)
    made = pl.pallas_call(
        round_kernel,
        out_shape=(pltpu.VMEM(block, F32), pltpu.VMEM((1, rows), F32), pltpu.VMEM(block, F32), pltpu.VMEM((1, rows), F32)),
        in_specs=[hbm] * 10,
        out_specs=(vmem,) * 4,
        scratch_shapes=[
            pltpu.VMEM(block, F32),
            pltpu.VMEM((1, rows), F32),
            pltpu.VMEM(block, F32),
            pltpu.VMEM((1, rows), F32),
            pltpu.VMEM((1, width), F32),
            pltpu.VMEM((owners, LANES), jnp.int32),
            pltpu.VMEM((owners, LANES), jnp.int32),
            pltpu.VMEM((1, edges), jnp.int32),
            pltpu.VMEM((1, edges), jnp.int32),
            pltpu.VMEM((1, negs), jnp.int32),
            pltpu.VMEM((2, chips, 2) + block, BF16),
            pltpu.VMEM((chips, 2, edges, rows), BF16),
            pltpu.VMEM((chips, 2, both, rows), BF16),
            pltpu.VMEM((1, edges), jnp.int32),
            pltpu.VMEM((1, both), jnp.int32),
            pltpu.VMEM((edges, LANES), jnp.int32),
            pltpu.VMEM((both, LANES), jnp.int32),
            pltpu.VMEM((width, edges), F32),
            pltpu.VMEM((width, both), F32),
            pltpu.VMEM((width, STRIP), F32),
            pltpu.VMEM((width, edges), BF16),
            pltpu.VMEM((edges, width), BF16),
            pltpu.VMEM((width, negs), BF16),
            pltpu.VMEM((edges, negs), BF16),
            pltpu.VMEM((1, edges), F32),
            pltpu.VMEM((width, edges), BF16),
            pltpu.VMEM((width, both), BF16),
            pltpu.VMEM((2, 3) + block, F32),
            pltpu.VMEM((2, 2, chips // 2) + block, BF16),
            pltpu.VMEM((2, 2, chips // 2) + block, BF16),
            pltpu.VMEM((2, chips) + block, BF16),
            pltpu.VMEM((2, chips) + block, BF16),
            pltpu.VMEM(block, BF16),
            pltpu.VMEM(block, BF16),
            pltpu.VMEM(block, F32),
            pltpu.VMEM((1, rows), F32),
            dma((10,)),
            dma((2, 2, chips // 2, 2)), dma((2, 2, chips // 2, 2)), dma((2, chips, 2)), dma((2, chips, 2)),
            dma((2, 2, chips // 2)), dma((2, 2, chips // 2)), dma((2, chips)), dma((2, chips)),
            dma((3,)), dma((3,)),
        ],
        compiler_params=pltpu.CompilerParams(
            collective_id=0, has_side_effects=True, vmem_limit_bytes=58 * 1024 * 1024
        ),
        name="bucket_round",
    )(
        left_rows.T, left_state.reshape(1, rows), right_rows.T, right_state.reshape(1, rows),
        relation.reshape(1, width), left_rows_wanted, right_rows_wanted,
        left_edge_position, right_edge_position, negative_position,
    )
    new_left, new_left_state, new_right, new_right_state = pl.pallas_call(
        place_kernel,
        out_shape=(a_block, a_state, a_block, a_state),
        in_specs=[vmem] * 4,
        out_specs=(hbm,) * 4,
        scratch_shapes=[dma((4,))],
        name="place",
    )(*(pltpu.with_memory_space_constraint(x, pltpu.VMEM) for x in made))
    return (new_left.T, new_left_state.reshape(rows), new_right.T, new_right_state.reshape(rows))


def solution(mesh):
    split = P(("dom", "edge"), None)
    return jax.shard_map(
        body,
        mesh=mesh,
        in_specs=(split, P(("dom", "edge")), split, P(("dom", "edge")), P(), split, split, split, split, split),
        out_specs=(split, P(("dom", "edge")), split, P(("dom", "edge"))),
        check_vma=False,
    )
```
